128 devices in a mesh: tm: 8 (over x, z_hi), tile: 16 (over y, z_lo, core).
Axes of the slice: x: 4, y: 4, z: 4 (z_hi: 2, z_lo: 2; z = z_hi * 2 + z_lo), core: 2. Of those that a mesh axis runs over, the one named last changes fastest.
Arguments:
- frames: bfloat16 [32, 64, 128, 256], P('tm', 'tile'), may hold values from -20 to 20
- first_gain: float32 [256], replicated, may hold values from 0.1 to 1.9
- first_bias: float32 [256], replicated, may hold values from -3 to 3
- first_weight: bfloat16 [3, 3, 3, 256, 256], replicated, may hold values from -0.078125 to 0.078125
- second_gain: float32 [256], replicated, may hold values from 0.1 to 1.9
- second_bias: float32 [256], replicated, may hold values from -3 to 3
- second_weight: bfloat16 [3, 3, 3, 256, 256], replicated, may hold values from -0.1875 to 0.1875
- latent_weight: bfloat16 [256, 16], replicated, may hold values from -0.375 to 0.375
Outputs:
- features: bfloat16 [32, 64, 128, 256], P('tm', 'tile')
- tokens: bfloat16 [32, 32, 4096], P('tm', None, 'tile')
The draws below stay inside these ranges and needn't reach their ends.
All inputs are finite; a program needn't handle non-finite values.
Results may differ from the reference program's by a relative error of at most 0.012.
Values may be sent and summed in bfloat16 or wider, within the bound.
A program may use at most 128 MiB of HBM per device.

```python
import jax
import jax.numpy as jnp
from jax import lax

C = 256
GROUPS = 32
LAT = 16
W = 128
NT = 32
NH = 64


def draw_frames(key, part):
    time_ramp = jnp.arange(NT, dtype=jnp.float32) / max(NT - 1, 1)
    row_ramp = jnp.arange(NH, dtype=jnp.float32) / max(NH - 1, 1)
    growth = jnp.exp(0.5 * jnp.log(3.0) * (time_ramp[:, None] + row_ramp[None, :]))[:, :, None, None]
    extent = (NT, NH, W, C)
    drawn = jax.random.truncated_normal(jax.random.fold_in(key, 13), -4.0, 4.0, extent, jnp.float32) * growth
    return drawn.astype(jnp.bfloat16)


def noise(stream_key, shape, width, reach, kind=jnp.bfloat16):
    result = width * jax.random.normal(stream_key, shape, jnp.float32)
    return jnp.clip(result, min=-reach, max=reach).astype(kind)


def setup_inputs(seed: int = 0) -> dict:
    splits = jax.random.split(jax.random.key(seed), 9)
    frames = draw_frames(jax.random.fold_in(splits[8], 71), 0)
    first_gain = jnp.clip(1.0 + 0.18 * jax.random.normal(splits[1], (C,), jnp.float32), 0.1, 1.9)
    first_bias = noise(splits[2], (C,), 0.5, 3.0, jnp.float32)
    first_weight = noise(splits[3], (3, 3, 3, C, C), (27 * C) ** -0.5, 0.078125)
    second_gain = jnp.clip(1.0 + 0.18 * jax.random.normal(splits[4], (C,), jnp.float32), 0.1, 1.9)
    second_bias = noise(splits[5], (C,), 0.5, 3.0, jnp.float32)
    second_weight = noise(splits[6], (3, 3, 3, C, C), (2.5 * (27 * C) ** -0.5), 0.1875)
    latent_weight = noise(splits[7], (C, LAT), C ** -0.5, 0.375)
    return {"frames": frames, "first_gain": first_gain, "first_bias": first_bias, "first_weight": first_weight, "second_gain": second_gain, "second_bias": second_bias, "second_weight": second_weight, "latent_weight": latent_weight}


def normalize(values, members, gain, bias):
    sums = lax.optimization_barrier(jnp.sum(values, axis=(0, 1, 2))).reshape(GROUPS, -1).sum(axis=1)
    squares = lax.optimization_barrier(jnp.sum(values * values, axis=(0, 1, 2))).reshape(GROUPS, -1).sum(axis=1)
    average = sums / members
    spread = squares / members - average * average
    inverse = lax.rsqrt(spread + 1e-06)
    factor = jnp.repeat(inverse, C // GROUPS) * gain
    offset = bias - jnp.repeat(average, C // GROUPS) * factor
    return jax.nn.silu(values * factor + offset).astype(jnp.bfloat16)

def causal_conv(active, kernel):
    convolved = lax.conv_general_dilated(active[None], kernel, (1, 1, 1), [(2, 0), (1, 1), (1, 1)], dimension_numbers=('NDHWC', 'DHWIO', 'NDHWC'), preferred_element_type=jnp.float32)
    return convolved[0]

def reference(frames, first_gain, first_bias, first_weight, second_gain, second_bias, second_weight, latent_weight):
    members = float(NT * NH * W * (C // GROUPS))
    inputs = frames.astype(jnp.float32)
    active = normalize(inputs, members, first_gain, first_bias)
    hidden = causal_conv(active, first_weight).astype(jnp.bfloat16)
    active = normalize(hidden.astype(jnp.float32), members, second_gain, second_bias)
    branch = causal_conv(active, second_weight)
    features = (inputs + branch).astype(jnp.bfloat16)
    latents = jnp.dot(features.reshape(-1, C), latent_weight, preferred_element_type=jnp.float32).astype(jnp.bfloat16)
    tokens = latents.reshape(NT, NH // 2, 2, W // 2, 2, LAT).transpose(0, 1, 3, 2, 4, 5).reshape(NT, NH // 2, -1)
    return (features, tokens)
```

```python
import functools

import jax
import jax.numpy as jnp
from jax import lax
from jax.experimental import pallas as pl
from jax.experimental.pallas import tpu as pltpu
from jax.sharding import PartitionSpec as P

GROUPS = 32
MESH = pl.DeviceIdType.MESH
F32, BF16 = jnp.float32, jnp.bfloat16
COLS, STEP, RUNS = 128, 16, 8


def iota(shape, dim):
    return lax.broadcasted_iota(jnp.int32, shape, dim)


def mm(a, b):
    return jnp.dot(a, b, preferred_element_type=F32)


def kernel(
    x, g1, b1, w1, g2, b2, w2, lw, feat, tok,
    raw, first, second, act, taps1, taps2, rows, spread, back, latent, outbox, inbox,
    part1, part2, part3, part4, load_sem, out_sem, hs1, hr1, hs2, hr2, as1, ar1, as2, ar2, as3, ar3, as4, ar4, ts, tr,
):
    tm, tile = lax.axis_index("tm"), lax.axis_index("tile")
    times, tiles = 8, 16
    core = lax.rem(tile, 2)

    def dev(t, h):
        return {"tm": t, "tile": h}

    def send(src, dst, s, r, device):
        return pltpu.make_async_remote_copy(
            src_ref=src, dst_ref=dst, send_sem=s, recv_sem=r, device_id=device, device_id_type=MESH
        )

    tile_peers = [dev(tm, lax.rem(tile + k, tiles)) for k in range(1, tiles)]
    time_peers = [dev(lax.rem(tm + k, times), tile) for k in range(1, times)]
    corners = [dev(lax.rem(tm + i, times), lax.rem(tile + j, tiles)) for i in (1, times - 1) for j in (1, tiles - 1)]
    peers = tile_peers + time_peers + corners

    loads = [pltpu.make_async_copy(x.at[f], raw.at[f], load_sem.at[f]) for f in range(4)]
    load_w1 = pltpu.make_async_copy(w1, taps1, load_sem.at[4])
    load_w2 = pltpu.make_async_copy(w2, taps2, load_sem.at[5])
    barrier = pltpu.get_barrier_semaphore()
    for f in (3, 2, 1, 0):
        loads[f].start()
    for peer in peers:
        pl.semaphore_signal(barrier, inc=1, device_id=peer, device_id_type=MESH)
    load_w1.start()
    load_w2.start()

    square = (COLS, COLS)
    a, b = iota(square, 0), iota(square, 1)
    spread[...] = (b == RUNS * (a % STEP) + a // STEP).astype(F32).astype(BF16)
    back[...] = (a == RUNS * (b % STEP) + b // STEP).astype(F32).astype(BF16)
    wide = (16, 256)
    repeat = (iota(wide, 0) == iota(wide, 1) % 16).astype(F32).astype(BF16)
    latent[...] = mm(lw[...], repeat).astype(BF16)

    def take(f):
        def row(r, sums):
            values = raw[f, r]
            first[2 + f, 1 + r] = mm(spread[...], values).astype(BF16)
            v = values.astype(F32).reshape(COLS // 8, 8, 256)
            return sums[0] + v.sum(axis=0), sums[1] + (v * v).sum(axis=0)

        return row

    zero = jnp.zeros((8, 256), F32)
    sums = (zero, zero)
    for f in (3, 2, 1, 0):
        loads[f].wait()
        sums = lax.fori_loop(0, 4, take(f), sums)
    pl.semaphore_wait(barrier, len(peers))

    class Halo:
        def __init__(self, buf, ss, rs):
            def copy(k, src, dst, device):
                return send(src, dst, ss.at[k], rs.at[k], device)

            right, left = dev(tm, tile + 1), dev(tm, tile - 1)
            self.rows = []
            for k, f in ((0, 4), (1, 2)):
                pair = pl.ds(f, 2)
                self.rows.append(
                    [
                        (copy(2 * k, buf.at[pair, 4], buf.at[pair, 0], right), tile < tiles - 1, tile > 0),
                        (copy(2 * k + 1, buf.at[pair, 1], buf.at[pair, 5], left), tile > 0, tile < tiles - 1),
                    ]
                )
            late, past, inner = pl.ds(4, 2), pl.ds(0, 2), pl.ds(1, 4)
            more, some = tm < times - 1, tm > 0
            self.time = [(copy(4, buf.at[late, inner], buf.at[past, inner], dev(tm + 1, tile)), more, some)]
            self.diagonal = [
                (
                    copy(5, buf.at[late, 4], buf.at[past, 0], dev(tm + 1, tile + 1)),
                    more & (core == 1) & (tile < tiles - 1),
                    some & (core == 0) & (tile > 0),
                ),
                (
                    copy(6, buf.at[late, 1], buf.at[past, 5], dev(tm + 1, tile - 1)),
                    more & (core == 0) & (tile > 0),
                    some & (core == 1) & (tile < tiles - 1),
                ),
            ]
            self.forward = [
                (copy(7, buf.at[past, 4], buf.at[past, 0], right), some & (core == 0), some & (core == 1)),
                (copy(8, buf.at[past, 1], buf.at[past, 5], left), some & (core == 1), some & (core == 0)),
            ]

    def start(copies):
        for copy, sends, _ in copies:
            pl.when(sends)(copy.start)

    def received(copies):
        for copy, _, receives in copies:
            pl.when(receives)(copy.wait_recv)

    def sent(copies):
        for copy, sends, _ in copies:
            pl.when(sends)(copy.wait_send)

    halo1, halo2 = Halo(first, hs1, hr1), Halo(second, hs2, hr2)
    start(halo1.rows[0] + halo1.rows[1] + halo1.time + halo1.diagonal)

    def over_devices(sums, wide_part, narrow_part, s1, r1, s2, r2):
        own = [jnp.sum(s, axis=0, keepdims=True) for s in sums]
        wide_part[0:1] = jnp.concatenate(own, axis=1)
        copies = [
            send(wide_part.at[pl.ds(0, 1)], wide_part.at[pl.ds(k, 1)], s1.at[k], r1.at[k], tile_peers[k - 1])
            for k in range(1, tiles)
        ]
        for copy in copies:
            copy.start()
        for copy in copies:
            copy.wait_recv()
        narrow_part[0:1] = jnp.sum(wide_part[...], axis=0, keepdims=True)
        more = [
            send(narrow_part.at[pl.ds(0, 1)], narrow_part.at[pl.ds(k, 1)], s2.at[k], r2.at[k], time_peers[k - 1])
            for k in range(1, times)
        ]
        for copy in more:
            copy.start()
        for copy in more:
            copy.wait_recv()
        return jnp.sum(narrow_part[...], axis=0, keepdims=True), copies + more

    members = float(32 * 64 * 128 * 8)

    def scales(total, gain, bias):
        shape = (256, 256)
        same = (iota(shape, 0) // 8 == iota(shape, 1) // 8).astype(F32)
        both = jnp.concatenate([total[:, :256], total[:, 256:], jnp.zeros((6, 256), F32)], axis=0)
        both = jnp.dot(both, same, preferred_element_type=F32, precision=lax.Precision.HIGHEST)
        average = both[0:1] / members
        spread_ = both[1:2] / members - average * average
        factor = lax.rsqrt(spread_ + 1e-06) * gain[...]
        return factor, bias[...] - average * factor

    def norm_row(buf, f, r, factor, offset):
        v = 0.5 * (buf[f, r].astype(F32) * factor + offset)
        y = v + v * jnp.tanh(v)
        at = f * 6 + r
        act[at, STEP : STEP + COLS] = y.astype(BF16)
        edge = iota((STEP, 256), 0)
        before = pltpu.roll(y[COLS - STEP :], 1, axis=0)
        after = pltpu.roll(y[:STEP], STEP - 1, axis=0)
        act[at, 0:STEP] = jnp.where(edge == 0, 0.0, before).astype(BF16)
        act[at, STEP + COLS :] = jnp.where(edge == STEP - 1, 0.0, after).astype(BF16)

    def norm_where(ok, buf, f, r, factor, offset):
        @pl.when(ok)
        def _():
            norm_row(buf, f, r, factor, offset)

        @pl.when(jnp.logical_not(ok))
        def _():
            act[f * 6 + r] = jnp.zeros((COLS + 2 * STEP, 256), BF16)

    def norm_own(buf, factor, offset):
        def some(i, _):
            norm_row(buf, 2 + i // 4, 1 + lax.rem(i, 4), factor, offset)
            return 0

        lax.fori_loop(0, 16, some, 0)

    def norm_sides(buf, f0, count, ok, factor, offset):
        def some(i, _):
            norm_where(ok & (tile > 0), buf, f0 + i, 0, factor, offset)
            norm_where(ok & (tile < tiles - 1), buf, f0 + i, 5, factor, offset)
            return 0

        lax.fori_loop(0, count, some, 0)

    def norm_past(buf, factor, offset):
        def some(i, _):
            norm_where(tm > 0, buf, i // 4, 1 + lax.rem(i, 4), factor, offset)
            return 0

        lax.fori_loop(0, 8, some, 0)

    def conv(taps, f):
        total = None
        for a in range(3):
            for b in range(3):
                at = pl.ds((f + a) * 6 + b, 4)
                piece = jnp.concatenate(
                    [act[at, STEP * c : STEP * c + COLS, :].reshape(4 * COLS, 256) for c in range(3)], axis=1
                )
                term = mm(piece, taps[a, b].reshape(768, 256))
                total = term if total is None else total + term
        return total

    def past_ready(halo, buf, factor, offset):
        received(halo.time)
        start(halo.forward)
        norm_past(buf, factor, offset)
        received(halo.diagonal + halo.forward)
        norm_sides(buf, 0, 2, tm > 0, factor, offset)

    total, reduced1 = over_devices(sums, part1, part2, as1, ar1, as2, ar2)
    factor1, offset1 = scales(total, g1, b1)
    norm_own(first, factor1, offset1)
    received(halo1.rows[0] + halo1.rows[1])
    norm_sides(first, 2, 4, True, factor1, offset1)
    load_w1.wait()

    def first_step(it, sums):
        @pl.when(it == 2)
        def _():
            start(halo2.rows[0] + halo2.time + halo2.diagonal)
            past_ready(halo1, first, factor1, offset1)

        f = lax.rem(it + 2, 4)
        hidden = conv(taps1, f).astype(BF16)
        second[2 + f, pl.ds(1, 4)] = hidden.reshape(4, COLS, 256)
        v = hidden.astype(F32).reshape(4 * COLS // 8, 8, 256)
        return sums[0] + v.sum(axis=0), sums[1] + (v * v).sum(axis=0)

    sums = lax.fori_loop(0, 4, first_step, (zero, zero))
    start(halo2.rows[1])

    total, reduced2 = over_devices(sums, part3, part4, as3, ar3, as4, ar4)
    factor2, offset2 = scales(total, g2, b2)
    norm_own(second, factor2, offset2)
    received(halo2.rows[0] + halo2.rows[1])
    norm_sides(second, 2, 4, True, factor2, offset2)
    load_w2.wait()

    def second_step(it, _):
        @pl.when(it == 2)
        def _():
            past_ready(halo2, second, factor2, offset2)

        f = lax.rem(it + 2, 4)
        branch = conv(taps2, f)
        frames = first[2 + f, pl.ds(1, 4)].reshape(4 * COLS, 256).astype(F32)
        features = (frames + branch).astype(BF16)
        for r in range(4):
            raw[f, r] = mm(back[...], features[r * COLS : (r + 1) * COLS]).astype(BF16)
        pltpu.make_async_copy(raw.at[f], feat.at[f], out_sem.at[f]).start()
        latents = mm(features, latent[...])
        lane = iota((STEP, 256), 1) // 16
        for i in range(2):
            block = jnp.zeros((STEP, 256), F32)
            for p in range(2):
                for s in range(RUNS):
                    at = (2 * i + p) * COLS + s * STEP
                    here = lane == 4 * (s // 2) + 2 * p + s % 2
                    block = jnp.where(here, latents[at : at + STEP], block)
            rows[pl.ds(pl.multiple_of((2 * f + i) * STEP, STEP), STEP)] = block
        return 0

    lax.fori_loop(0, 4, second_step, 0)

    turn = (b == (a % 8) * 16 + a // 8).astype(F32).astype(BF16)
    outbox[...] = mm(turn, rows[...].astype(BF16)).reshape(16, 8, 256)
    copies = []
    for k in range(1, tiles):
        to = lax.rem(tile + k, tiles)
        copies.append(send(outbox.at[to], inbox.at[tile], ts.at[k], tr.at[k], dev(tm, to)))
    for copy in copies:
        copy.start()
    inbox[tile] = outbox[tile]
    turn = (b == ((a % 32) // 2) * 8 + (a // 32) * 2 + a % 2).astype(F32).astype(BF16)
    for k in range(1, tiles):
        source = lax.rem(tile + tiles - k, tiles)
        send(outbox.at[source], inbox.at[source], ts.at[k], tr.at[k], dev(tm, source)).wait_recv()
    tok[...] = mm(turn, inbox[...].reshape(128, 256).astype(BF16)).astype(BF16).reshape(4, 32, 256)
    for f in range(4):
        pltpu.make_async_copy(raw.at[f], feat.at[f], out_sem.at[f]).wait()
    for copy in copies + reduced1 + reduced2:
        copy.wait_send()
    for halo in (halo1, halo2):
        sent(halo.rows[0] + halo.rows[1] + halo.time + halo.diagonal + halo.forward)


def body(frames, g1, b1, w1, g2, b2, w2, lw):
    hbm, vmem = pl.BlockSpec(memory_space=pltpu.HBM), pl.BlockSpec(memory_space=pltpu.VMEM)
    dma = pltpu.SemaphoreType.DMA
    return pl.pallas_call(
        kernel,
        out_shape=[
            jax.ShapeDtypeStruct((4, 4, 128, 256), BF16),
            jax.ShapeDtypeStruct((4, 32, 256), BF16),
        ],
        in_specs=[hbm, vmem, vmem, hbm, vmem, vmem, hbm, vmem],
        out_specs=[hbm, vmem],
        scratch_shapes=[
            pltpu.VMEM((4, 4, 128, 256), BF16),
            pltpu.VMEM((6, 6, 128, 256), BF16),
            pltpu.VMEM((6, 6, 128, 256), BF16),
            pltpu.VMEM((36, 160, 256), BF16),
            pltpu.VMEM((3, 3, 3, 256, 256), BF16),
            pltpu.VMEM((3, 3, 3, 256, 256), BF16),
            pltpu.VMEM((128, 256), F32),
            pltpu.VMEM((128, 128), BF16),
            pltpu.VMEM((128, 128), BF16),
            pltpu.VMEM((256, 256), BF16),
            pltpu.VMEM((16, 8, 256), F32),
            pltpu.VMEM((16, 8, 256), F32),
            pltpu.VMEM((16, 512), F32),
            pltpu.VMEM((8, 512), F32),
            pltpu.VMEM((16, 512), F32),
            pltpu.VMEM((8, 512), F32),
            dma((6,)),
            dma((4,)),
        ]
        + [dma((9,))] * 4
        + [dma((16,)), dma((16,)), dma((8,)), dma((8,))] * 2
        + [dma((16,)), dma((16,))],
        compiler_params=pltpu.CompilerParams(
            collective_id=0, has_side_effects=True, vmem_limit_bytes=50 * 2**20
        ),
    )(frames, g1.reshape(1, 256), b1.reshape(1, 256), w1, g2.reshape(1, 256), b2.reshape(1, 256), w2, lw)


def solution(mesh):
    return jax.shard_map(
        body,
        mesh=mesh,
        in_specs=(P("tm", "tile", None, None), P(), P(), P(), P(), P(), P(), P()),
        out_specs=(P("tm", "tile", None, None), P("tm", None, "tile")),
        check_vma=False,
    )
```

```python
import functools

import jax
import jax.numpy as jnp
from jax import lax
from jax.experimental import pallas as pl
from jax.experimental.pallas import tpu as pltpu
from jax.sharding import PartitionSpec as P

GROUPS = 32
MESH = pl.DeviceIdType.MESH
F32, BF16 = jnp.float32, jnp.bfloat16
COLS, STEP, RUNS = 128, 16, 8


def iota(shape, dim):
    return lax.broadcasted_iota(jnp.int32, shape, dim)


def mm(a, b):
    return jnp.dot(a, b, preferred_element_type=F32)


def kernel(
    x, params, w1, w2, feat, tok,
    raw, final, first, second, act, mixed, acc, taps1, taps2, blend1, blend2, rows, spread, back, latent, groups, outbox, inbox,
    part1, part2, part3, part4, load_sem, out_sem, hs1, hr1, hs2, hr2, as1, ar1, as2, ar2, as3, ar3, as4, ar4, ts, tr,
):
    tm, tile = lax.axis_index("tm"), lax.axis_index("tile")
    times, tiles = 8, 16
    core = lax.rem(tile, 2)
    cx, cy, cz = tm // 2, tile // 4, lax.rem(tm, 2) * 2 + lax.rem(tile // 2, 2)

    def dev(t, h):
        return {"tm": t, "tile": h}

    def at_chip(i, j, k, c):
        return dev(i * 2 + k // 2, j * 4 + lax.rem(k, 2) * 2 + c)

    def send(src, dst, s, r, device):
        return pltpu.make_async_remote_copy(
            src_ref=src, dst_ref=dst, send_sem=s, recv_sem=r, device_id=device, device_id_type=MESH
        )

    tile_peers = [dev(tm, lax.rem(tile + k, tiles)) for k in range(1, tiles)]
    near_peers = [
        at_chip(cx, cy, lax.rem(cz + k // 2, 4), lax.rem(core + k % 2, 2)) for k in (4, 5, 2, 3, 6, 7, 1)
    ]
    far_peers = [
        at_chip(lax.rem(cx + k // 4, 4), lax.rem(cy + k % 4, 4), cz, core) for k in (10, 9, 11, 6, 14, 2, 8, 5, 7, 13, 15, 1, 3, 4, 12)
    ]
    sides = [
        dev(lax.rem(tm + i, times), lax.rem(tile + j, tiles)) for i in (1, times - 1) for j in (0, 1, tiles - 1)
    ]
    peers = tile_peers + near_peers + far_peers + sides

    loads = [pltpu.make_async_copy(x.at[f], raw.at[f], load_sem.at[f]) for f in range(4)]
    load_w1 = pltpu.make_async_copy(w1, taps1, load_sem.at[4])
    load_w2 = pltpu.make_async_copy(w2, taps2, load_sem.at[5])
    barrier = pltpu.get_barrier_semaphore()
    for f in range(4):
        loads[f].start()
    for peer in peers:
        pl.semaphore_signal(barrier, inc=1, device_id=peer, device_id_type=MESH)
    load_w1.start()

    zero = jnp.zeros((8, 256), F32)
    sums = (zero, zero)
    for f in range(4):
        loads[f].wait()

        def add_row(r, sums, f=f):
            v = raw[f, r].astype(F32).reshape(COLS // 8, 8, 256)
            return sums[0] + v.sum(axis=0), sums[1] + (v * v).sum(axis=0)

        sums = lax.fori_loop(0, 4, add_row, sums, unroll=True)

    class Totals:
        def __init__(self, wide_part, narrow_part, s1, r1, s2, r2):
            self.parts = (wide_part, narrow_part)
            self.copies = [
                [
                    send(part.at[pl.ds(0, 1)], part.at[pl.ds(k + 1, 1)], s.at[k], r.at[k], peer)
                    for k, peer in enumerate(group)
                ]
                for part, s, r, group in ((wide_part, s1, r1, near_peers), (narrow_part, s2, r2, far_peers))
            ]

        def begin(self, sums):
            own = [jnp.sum(s, axis=0, keepdims=True) for s in sums]
            self.parts[0][0:1] = jnp.concatenate(own, axis=1)
            for copy in self.copies[0]:
                copy.start()

        def middle(self):
            for copy in self.copies[0]:
                copy.wait_recv()
            self.parts[1][0:1] = jnp.sum(self.parts[0][...], axis=0, keepdims=True)
            for copy in self.copies[1]:
                copy.start()

        def end(self):
            for copy in self.copies[1]:
                copy.wait_recv()
            return jnp.sum(self.parts[1][...], axis=0, keepdims=True)

        def sent(self):
            for copy in self.copies[0] + self.copies[1]:
                copy.wait_send()

    totals1 = Totals(part1, part2, as1, ar1, as2, ar2)
    totals2 = Totals(part3, part4, as3, ar3, as4, ar4)

    class Halo:
        def __init__(self, buf, ss, rs):
            def copy(k, src, dst, device):
                return send(src, dst, ss.at[k], rs.at[k], device)

            right, left, later = dev(tm, tile + 1), dev(tm, tile - 1), dev(tm + 1, tile)
            more, some = tm < times - 1, tm > 0
            self.rows, self.edge, self.rest, self.forward = {}, {}, {}, {}
            for k, f in ((0, 4), (1, 2)):
                pair = pl.ds(f, 2)
                self.rows[f] = [
                    (copy(2 * k, buf.at[pair, 4], buf.at[pair, 0], right), tile < tiles - 1, tile > 0),
                    (copy(2 * k + 1, buf.at[pair, 1], buf.at[pair, 5], left), tile > 0, tile < tiles - 1),
                ]
            late, past = pl.ds(4, 2), pl.ds(0, 2)
            edge, rest = 4 - 3 * core, pl.ds(1 + core, 3)
            self.edge = [(copy(4, buf.at[late, edge], buf.at[past, edge], later), more, some)]
            for f in (1, 0):
                self.rest[f] = [(copy(5 + f, buf.at[4 + f, rest], buf.at[f, rest], later), more, some)]
            self.diagonal = [
                (
                    copy(7, buf.at[late, 4], buf.at[past, 0], dev(tm + 1, tile + 1)),
                    more & (core == 1) & (tile < tiles - 1),
                    some & (core == 0) & (tile > 0),
                ),
                (
                    copy(8, buf.at[late, 1], buf.at[past, 5], dev(tm + 1, tile - 1)),
                    more & (core == 0) & (tile > 0),
                    some & (core == 1) & (tile < tiles - 1),
                ),
            ]
            self.forward = [
                (copy(9, buf.at[past, 4], buf.at[past, 0], right), some & (core == 0), some & (core == 1)),
                (copy(10, buf.at[past, 1], buf.at[past, 5], left), some & (core == 1), some & (core == 0)),
            ]
            self.all = self.rows[4] + self.rows[2] + self.edge + self.rest[1] + self.rest[0]
            self.all = self.all + self.diagonal + self.forward

    def start(copies):
        for copy, sends, _ in copies:
            pl.when(sends)(copy.start)

    def received(copies):
        for copy, _, receives in copies:
            pl.when(receives)(copy.wait_recv)

    def sent(copies):
        for copy, sends, _ in copies:
            pl.when(sends)(copy.wait_send)

    halo1, halo2 = Halo(first, hs1, hr1), Halo(second, hs2, hr2)

    pl.semaphore_wait(barrier, len(peers))
    totals1.begin(sums)

    square = (COLS, COLS)
    a, b = iota(square, 0), iota(square, 1)
    spread[...] = (b == RUNS * (a % STEP) + a // STEP).astype(F32).astype(BF16)
    back[...] = (a == RUNS * (b % STEP) + b // STEP).astype(F32).astype(BF16)

    def place(i, _):
        f, r = i // 4, lax.rem(i, 4)
        first[2 + f, 1 + r] = mm(spread[...], raw[f, r]).astype(BF16)
        return 0

    lax.fori_loop(0, 16, place, 0, unroll=4)
    start(halo1.rows[4] + halo1.rows[2])
    load_w2.start()

    wide = (16, 256)
    repeat = (iota(wide, 0) == iota(wide, 1) % 16).astype(F32).astype(BF16)
    latent[...] = lax.dot_general(
        params[0:16].astype(BF16), repeat, (((0,), (0,)), ((), ())), preferred_element_type=F32
    ).astype(BF16)
    shape = (256, 256)
    groups[...] = (iota(shape, 0) // 8 == iota(shape, 1) // 8).astype(F32).astype(BF16)
    none = jnp.zeros((COLS + 2 * STEP, 256), BF16)
    for outside, r in ((tile == 0, 0), (tile == tiles - 1, 5)):

        @pl.when(outside)
        def _(r=r):
            for f in range(6):
                act[f * 6 + r] = none

    @pl.when(tm == 0)
    def _():
        for k in range(12):
            act[k] = none

    def blend(taps, into):
        def some(k, _):
            b, c = k // 3, lax.rem(k, 3)
            outer = 0.5 * (taps[0, b, c].astype(F32) + taps[2, b, c].astype(F32))
            inner = 0.5 * taps[1, b, c].astype(F32)
            into[0, b, c] = (outer + inner).astype(BF16)
            into[1, b, c] = (outer - inner).astype(BF16)
            return 0

        lax.fori_loop(0, 9, some, 0)

    load_w1.wait()
    blend(taps1, blend1)
    totals1.middle()
    start(halo1.edge + halo1.diagonal + halo1.rest[1] + halo1.rest[0])
    load_w2.wait()
    blend(taps2, blend2)

    members = float(32 * 64 * 128 * 8)

    def scales(total, gain, bias):
        both = jnp.concatenate([total[:, :256], total[:, 256:]], axis=0)
        high = both.astype(BF16).astype(F32)
        middle = (both - high).astype(BF16).astype(F32)
        low = both - high - middle
        split = jnp.concatenate([high, middle, low, jnp.zeros((2, 256), F32)], axis=0).astype(BF16)
        split = mm(split, groups[...])
        both = split[0:2] + split[2:4] + split[4:6]
        average = both[0:1] / members
        variance = both[1:2] / members - average * average
        factor = lax.rsqrt(variance + 1e-06) * gain
        return 0.5 * factor, 0.5 * (bias - average * factor)

    def norm_row(buf, f, r, scale):
        v = buf[f, r].astype(F32) * scale[0] + scale[1]
        y = v + v * jnp.tanh(v)
        at = f * 6 + r
        act[at, STEP : STEP + COLS] = y.astype(BF16)
        edge = iota((STEP, 256), 0)
        before = pltpu.roll(y[COLS - STEP :], 1, axis=0)
        after = pltpu.roll(y[:STEP], STEP - 1, axis=0)
        act[at, 0:STEP] = jnp.where(edge == 0, 0.0, before).astype(BF16)
        act[at, STEP + COLS :] = jnp.where(edge == STEP - 1, 0.0, after).astype(BF16)

    def norm_own(buf, scale):
        def some(i, _):
            norm_row(buf, 2 + i // 4, 1 + lax.rem(i, 4), scale)
            return 0

        lax.fori_loop(0, 16, some, 0, unroll=8)

    def norm_sides(buf, scale):
        for inside, r in ((tile > 0, 0), (tile < tiles - 1, 5)):

            @pl.when(inside)
            def _(r=r):
                for f in range(2, 6):
                    norm_row(buf, f, r, scale)

    def norm_past(buf, f, scale):
        @pl.when(tm > 0)
        def _():
            for r in range(1, 5):
                norm_row(buf, f, r, scale)

        for inside, r in ((tile > 0, 0), (tile < tiles - 1, 5)):

            @pl.when(inside & (tm > 0))
            def _(r=r):
                norm_row(buf, f, r, scale)

    def mix(q):
        def some(r, _):
            d = [act[(2 - 2 * q + i) * 6 + r] for i in range(4)]
            mixed[r] = d[0] - d[2]
            mixed[6 + r] = d[1] + d[2]
            mixed[12 + r] = d[2] - d[1]
            mixed[18 + r] = d[1] - d[3]
            return 0

        lax.fori_loop(0, 6, some, 0, unroll=2)

    def product(taps, j):
        total = None
        for b in range(3):
            at = pl.ds(j * 6 + b, 4)
            piece = jnp.concatenate(
                [mixed[at, STEP * c : STEP * c + COLS, :].reshape(4 * COLS, 256) for c in range(3)], axis=1
            )
            term = mm(piece, taps[b].reshape(768, 256))
            total = term if total is None else total + term
        return total

    def direct(taps, units):
        total = None
        for o, a in units:
            for b in range(3):
                at = pl.ds((o + a) * 6 + b, 4)
                piece = jnp.concatenate(
                    [act[at, STEP * c : STEP * c + COLS, :].reshape(4 * COLS, 256) for c in range(3)], axis=1
                )
                term = mm(piece, taps[a, b].reshape(768, 256))
                total = term if total is None else total + term
        return total

    def conv(taps, blended, halo, buf, scale, done, between, arrived):
        mix(0)
        m1, m2 = product(blended.at[0], 1), product(blended.at[1], 2)
        y0, y1 = m1 + m2, m1 - m2
        acc[0] = y0 + product(taps.at[0], 0)
        acc[1] = y1 - product(taps.at[2], 3)
        carry = done(2, 0, (zero, zero))
        carry = done(2, 1, carry)
        between()
        acc[0] = direct(taps, ((0, 2),))
        acc[1] = direct(taps, ((1, 1), (1, 2)))
        received(halo.diagonal + halo.forward + halo.rest[1])
        norm_past(buf, 1, scale)
        received(halo.rest[0])
        arrived()
        norm_past(buf, 0, scale)
        acc[1] += direct(taps, ((1, 0),))
        acc[0] += direct(taps, ((0, 1), (0, 0)))
        return done(0, 1, done(0, 0, carry))

    scale = scales(totals1.end(), params[16:17], params[17:18])
    norm_own(first, scale)
    received(halo1.rows[4] + halo1.rows[2])
    norm_sides(first, scale)
    received(halo1.edge)
    start(halo1.forward)

    def keep(o, half, sums):
        hidden = acc[half].astype(BF16)
        second[2 + o + half, pl.ds(1, 4)] = hidden.reshape(4, COLS, 256)
        v = hidden.astype(F32).reshape(4 * COLS // 8, 8, 256)
        return sums[0] + v.sum(axis=0), sums[1] + (v * v).sum(axis=0)

    sums = conv(
        taps1, blend1, halo1, first, scale, keep, lambda: None, lambda: start(halo2.rows[4] + halo2.edge + halo2.diagonal)
    )

    totals2.begin(sums)
    start(halo2.rows[2])
    totals2.middle()
    start(halo2.rest[1] + halo2.rest[0])
    scale = scales(totals2.end(), params[18:19], params[19:20])
    norm_own(second, scale)
    received(halo2.rows[4] + halo2.rows[2])
    norm_sides(second, scale)
    received(halo2.edge)
    start(halo2.forward)

    def finish_latents(o, half):
        frames = first[2 + o, pl.ds(1, 4)].reshape(4 * COLS, 256).astype(F32)
        features = (frames + acc[half]).astype(BF16)
        final[o] = features.reshape(4, COLS, 256)
        latents = mm(features, latent[...])
        lane = iota((STEP, 256), 1) // 16
        for i in range(2):
            block = jnp.zeros((STEP, 256), F32)
            for p in range(2):
                for s in range(RUNS):
                    at = (2 * i + p) * COLS + s * STEP
                    here = lane == 4 * (s // 2) + 2 * p + s % 2
                    block = jnp.where(here, latents[at : at + STEP], block)
            rows[pl.ds(pl.multiple_of((2 * o + i) * STEP, STEP), STEP)] = block

    def finish_features(o):
        for r in range(4):
            raw[o, r] = mm(back[...], final[o, r]).astype(BF16)
        pltpu.make_async_copy(raw.at[o], feat.at[o], out_sem.at[o]).start()

    def finish(o, half, carry):
        finish_latents(o + half, half)
        return carry

    def finish_early():
        finish_features(3)
        finish_features(2)

    conv(taps2, blend2, halo2, second, scale, finish, finish_early, lambda: None)

    turn = (b == (a % 8) * 16 + a // 8).astype(F32).astype(BF16)
    outbox[...] = mm(turn, rows[...].astype(BF16)).reshape(16, 8, 256)
    copies = []
    for k in range(1, tiles):
        to = lax.rem(tile + k, tiles)
        copies.append(send(outbox.at[to], inbox.at[tile], ts.at[k], tr.at[k], dev(tm, to)))
    for copy in copies:
        copy.start()

    finish_features(1)
    finish_features(0)
    inbox[tile] = outbox[tile]
    turn = (b == ((a % 32) // 2) * 8 + (a // 32) * 2 + a % 2).astype(F32).astype(BF16)
    for k in range(1, tiles):
        source = lax.rem(tile + tiles - k, tiles)
        send(outbox.at[source], inbox.at[source], ts.at[k], tr.at[k], dev(tm, source)).wait_recv()
    tok[...] = mm(turn, inbox[...].reshape(128, 256).astype(BF16)).astype(BF16).reshape(4, 32, 256)
    for f in range(4):
        pltpu.make_async_copy(raw.at[f], feat.at[f], out_sem.at[f]).wait()
    for copy in copies:
        copy.wait_send()
    totals1.sent()
    totals2.sent()
    sent(halo1.all + halo2.all)


def body(frames, g1, b1, w1, g2, b2, w2, lw):
    hbm, vmem = pl.BlockSpec(memory_space=pltpu.HBM), pl.BlockSpec(memory_space=pltpu.VMEM)
    dma = pltpu.SemaphoreType.DMA
    params = jnp.concatenate([lw.T.astype(F32)] + [v.reshape(1, 256) for v in (g1, b1, g2, b2)], axis=0)
    return pl.pallas_call(
        kernel,
        out_shape=[
            jax.ShapeDtypeStruct((4, 4, 128, 256), BF16),
            jax.ShapeDtypeStruct((4, 32, 256), BF16),
        ],
        in_specs=[hbm, vmem, hbm, hbm],
        out_specs=[hbm, vmem],
        scratch_shapes=[
            pltpu.VMEM((4, 4, 128, 256), BF16),
            pltpu.VMEM((4, 4, 128, 256), BF16),
            pltpu.VMEM((6, 6, 128, 256), BF16),
            pltpu.VMEM((6, 6, 128, 256), BF16),
            pltpu.VMEM((36, 160, 256), BF16),
            pltpu.VMEM((24, 160, 256), BF16),
            pltpu.VMEM((2, 512, 256), F32),
            pltpu.VMEM((3, 3, 3, 256, 256), BF16),
            pltpu.VMEM((3, 3, 3, 256, 256), BF16),
            pltpu.VMEM((2, 3, 3, 256, 256), BF16),
            pltpu.VMEM((2, 3, 3, 256, 256), BF16),
            pltpu.VMEM((128, 256), F32),
            pltpu.VMEM((128, 128), BF16),
            pltpu.VMEM((128, 128), BF16),
            pltpu.VMEM((256, 256), BF16),
            pltpu.VMEM((256, 256), BF16),
            pltpu.VMEM((16, 8, 256), F32),
            pltpu.VMEM((16, 8, 256), F32),
            pltpu.VMEM((8, 512), F32),
            pltpu.VMEM((16, 512), F32),
            pltpu.VMEM((8, 512), F32),
            pltpu.VMEM((16, 512), F32),
            dma((11,)),
            dma((4,)),
        ]
        + [dma((11,))] * 4
        + [dma((7,)), dma((7,)), dma((15,)), dma((15,))] * 2
        + [dma((16,)), dma((16,))],
        compiler_params=pltpu.CompilerParams(
            collective_id=0, has_side_effects=True, vmem_limit_bytes=54000 * 2**10
        ),
    )(frames, params, w1, w2)


def solution(mesh):
    return jax.shard_map(
        body,
        mesh=mesh,
        in_specs=(P("tm", "tile", None, None), P(), P(), P(), P(), P(), P(), P()),
        out_specs=(P("tm", "tile", None, None), P("tm", None, "tile")),
        check_vma=False,
    )
```

```python
import functools

import jax
import jax.numpy as jnp
from jax import lax
from jax.experimental import pallas as pl
from jax.experimental.pallas import tpu as pltpu
from jax.sharding import PartitionSpec as P

GROUPS = 32
MESH = pl.DeviceIdType.MESH
F32, BF16 = jnp.float32, jnp.bfloat16
COLS, STEP, RUNS = 128, 16, 8


def iota(shape, dim):
    return lax.broadcasted_iota(jnp.int32, shape, dim)


def mm(a, b):
    return jnp.dot(a, b, preferred_element_type=F32)


def kernel(
    x, params, w1, w2, feat, tok,
    raw, final, first, second, act, mixed, acc, taps1, taps2, blend1, blend2, rows, spread, back, latent, groups, outbox, inbox,
    part1, part2, part3, part4, load_sem, hs1, hr1, hs2, hr2, as1, ar1, as2, ar2, as3, ar3, as4, ar4, ts, tr,
):
    tm, tile = lax.axis_index("tm"), lax.axis_index("tile")
    times, tiles = 8, 16
    core = lax.rem(tile, 2)
    cx, cy, cz = tm // 2, tile // 4, lax.rem(tm, 2) * 2 + lax.rem(tile // 2, 2)

    def dev(t, h):
        return {"tm": t, "tile": h}

    def at_chip(i, j, k, c):
        return dev(i * 2 + k // 2, j * 4 + lax.rem(k, 2) * 2 + c)

    def send(src, dst, s, r, device):
        return pltpu.make_async_remote_copy(
            src_ref=src, dst_ref=dst, send_sem=s, recv_sem=r, device_id=device, device_id_type=MESH
        )

    tile_peers = [dev(tm, lax.rem(tile + k, tiles)) for k in range(1, tiles)]
    near_peers = [
        at_chip(cx, cy, lax.rem(cz + k // 2, 4), lax.rem(core + k % 2, 2)) for k in (4, 5, 2, 3, 6, 7, 1)
    ]
    far_peers = [
        at_chip(lax.rem(cx + k // 4, 4), lax.rem(cy + k % 4, 4), cz, core) for k in (10, 9, 11, 6, 14, 2, 8, 5, 7, 13, 15, 1, 3, 4, 12)
    ]
    sides = [
        dev(lax.rem(tm + i, times), lax.rem(tile + j, tiles)) for i in (1, times - 1) for j in (0, 1, tiles - 1)
    ]
    peers = tile_peers + near_peers + far_peers + sides

    loads = [pltpu.make_async_copy(x.at[f], raw.at[f], load_sem.at[f]) for f in range(4)]
    load_w1 = pltpu.make_async_copy(w1, taps1, load_sem.at[4])
    load_w2 = pltpu.make_async_copy(w2, taps2, load_sem.at[5])
    barrier = pltpu.get_barrier_semaphore()
    for f in range(4):
        loads[f].start()
    for peer in peers:
        pl.semaphore_signal(barrier, inc=1, device_id=peer, device_id_type=MESH)
    load_w1.start()

    zero = jnp.zeros((8, 256), F32)
    sums = (zero, zero)
    for f in range(4):
        loads[f].wait()

        def add_row(r, sums, f=f):
            v = raw[f, r].astype(F32).reshape(COLS // 8, 8, 256)
            return sums[0] + v.sum(axis=0), sums[1] + (v * v).sum(axis=0)

        sums = lax.fori_loop(0, 4, add_row, sums, unroll=True)

    class Totals:
        def __init__(self, wide_part, narrow_part, s1, r1, s2, r2):
            self.parts = (wide_part, narrow_part)
            self.copies = [
                [
                    send(part.at[pl.ds(0, 1)], part.at[pl.ds(k + 1, 1)], s.at[k], r.at[k], peer)
                    for k, peer in enumerate(group)
                ]
                for part, s, r, group in ((wide_part, s1, r1, near_peers), (narrow_part, s2, r2, far_peers))
            ]

        def begin(self, sums):
            own = [jnp.sum(s, axis=0, keepdims=True) for s in sums]
            self.parts[0][0:1] = jnp.concatenate(own, axis=1)
            for copy in self.copies[0]:
                copy.start()

        def middle(self):
            for copy in self.copies[0]:
                copy.wait_recv()
            self.parts[1][0:1] = jnp.sum(self.parts[0][...], axis=0, keepdims=True)
            for copy in self.copies[1]:
                copy.start()

        def end(self):
            for copy in self.copies[1]:
                copy.wait_recv()
            return jnp.sum(self.parts[1][...], axis=0, keepdims=True)

        def sent(self):
            for copy in self.copies[0] + self.copies[1]:
                copy.wait_send()

    totals1 = Totals(part1, part2, as1, ar1, as2, ar2)
    totals2 = Totals(part3, part4, as3, ar3, as4, ar4)

    class Halo:
        def __init__(self, buf, ss, rs):
            def copy(k, src, dst, device):
                return send(src, dst, ss.at[k], rs.at[k], device)

            right, left, later = dev(tm, tile + 1), dev(tm, tile - 1), dev(tm + 1, tile)
            more, some = tm < times - 1, tm > 0
            self.rows, self.edge, self.rest, self.forward = {}, {}, {}, {}
            for k, f in ((0, 4), (1, 2)):
                pair = pl.ds(f, 2)
                self.rows[f] = [
                    (copy(2 * k, buf.at[pair, 4], buf.at[pair, 0], right), tile < tiles - 1, tile > 0),
                    (copy(2 * k + 1, buf.at[pair, 1], buf.at[pair, 5], left), tile > 0, tile < tiles - 1),
                ]
            late, past = pl.ds(4, 2), pl.ds(0, 2)
            edge, rest = 4 - 3 * core, pl.ds(1 + core, 3)
            self.edge = [(copy(4, buf.at[late, edge], buf.at[past, edge], later), more, some)]
            for f in (1, 0):
                self.rest[f] = [(copy(5 + f, buf.at[4 + f, rest], buf.at[f, rest], later), more, some)]
            self.diagonal = [
                (
                    copy(7, buf.at[late, 4], buf.at[past, 0], dev(tm + 1, tile + 1)),
                    more & (core == 1) & (tile < tiles - 1),
                    some & (core == 0) & (tile > 0),
                ),
                (
                    copy(8, buf.at[late, 1], buf.at[past, 5], dev(tm + 1, tile - 1)),
                    more & (core == 0) & (tile > 0),
                    some & (core == 1) & (tile < tiles - 1),
                ),
            ]
            self.forward = [
                (copy(9, buf.at[past, 4], buf.at[past, 0], right), some & (core == 0), some & (core == 1)),
                (copy(10, buf.at[past, 1], buf.at[past, 5], left), some & (core == 1), some & (core == 0)),
            ]
            self.all = self.rows[4] + self.rows[2] + self.edge + self.rest[1] + self.rest[0]
            self.all = self.all + self.diagonal + self.forward

    def start(copies):
        for copy, sends, _ in copies:
            pl.when(sends)(copy.start)

    def received(copies):
        for copy, _, receives in copies:
            pl.when(receives)(copy.wait_recv)

    def sent(copies):
        for copy, sends, _ in copies:
            pl.when(sends)(copy.wait_send)

    halo1, halo2 = Halo(first, hs1, hr1), Halo(second, hs2, hr2)

    pl.semaphore_wait(barrier, len(peers))
    totals1.begin(sums)

    square = (COLS, COLS)
    a, b = iota(square, 0), iota(square, 1)
    spread[...] = (b == RUNS * (a % STEP) + a // STEP).astype(F32).astype(BF16)
    back[...] = (a == RUNS * (b % STEP) + b // STEP).astype(F32).astype(BF16)

    def place(i, _):
        f, r = i // 4, lax.rem(i, 4)
        first[2 + f, 1 + r] = mm(spread[...], raw[f, r]).astype(BF16)
        return 0

    lax.fori_loop(0, 16, place, 0, unroll=4)
    start(halo1.rows[4] + halo1.rows[2])
    load_w2.start()

    wide = (16, 256)
    repeat = (iota(wide, 0) == iota(wide, 1) % 16).astype(F32).astype(BF16)
    latent[...] = lax.dot_general(
        params[0:16].astype(BF16), repeat, (((0,), (0,)), ((), ())), preferred_element_type=F32
    ).astype(BF16)
    shape = (256, 256)
    groups[...] = (iota(shape, 0) // 8 == iota(shape, 1) // 8).astype(F32).astype(BF16)
    none = jnp.zeros((COLS + 2 * STEP, 256), BF16)
    for outside, r in ((tile == 0, 0), (tile == tiles - 1, 5)):

        @pl.when(outside)
        def _(r=r):
            for f in range(6):
                act[f * 6 + r] = none

    @pl.when(tm == 0)
    def _():
        for k in range(12):
            act[k] = none

    def blend(taps, into):
        def some(k, _):
            b, c = k // 3, lax.rem(k, 3)
            outer = 0.5 * (taps[0, b, c].astype(F32) + taps[2, b, c].astype(F32))
            inner = 0.5 * taps[1, b, c].astype(F32)
            into[0, b, c] = (outer + inner).astype(BF16)
            into[1, b, c] = (outer - inner).astype(BF16)
            return 0

        lax.fori_loop(0, 9, some, 0)

    load_w1.wait()
    blend(taps1, blend1)
    totals1.middle()
    start(halo1.edge + halo1.diagonal + halo1.rest[1] + halo1.rest[0])
    load_w2.wait()
    blend(taps2, blend2)

    members = float(32 * 64 * 128 * 8)

    def scales(total, gain, bias):
        both = jnp.concatenate([total[:, :256], total[:, 256:]], axis=0)
        high = both.astype(BF16).astype(F32)
        middle = (both - high).astype(BF16).astype(F32)
        low = both - high - middle
        split = jnp.concatenate([high, middle, low, jnp.zeros((2, 256), F32)], axis=0).astype(BF16)
        split = mm(split, groups[...])
        both = split[0:2] + split[2:4] + split[4:6]
        average = both[0:1] / members
        variance = both[1:2] / members - average * average
        factor = lax.rsqrt(variance + 1e-06) * gain
        return 0.5 * factor, 0.5 * (bias - average * factor)

    def norm_row(buf, f, r, scale):
        v = buf[f, r].astype(F32) * scale[0] + scale[1]
        y = v + v * jnp.tanh(v)
        at = f * 6 + r
        act[at, STEP : STEP + COLS] = y.astype(BF16)
        edge = iota((STEP, 256), 0)
        before = pltpu.roll(y[COLS - STEP :], 1, axis=0)
        after = pltpu.roll(y[:STEP], STEP - 1, axis=0)
        act[at, 0:STEP] = jnp.where(edge == 0, 0.0, before).astype(BF16)
        act[at, STEP + COLS :] = jnp.where(edge == STEP - 1, 0.0, after).astype(BF16)

    def norm_own(buf, scale):
        def some(i, _):
            norm_row(buf, 2 + i // 4, 1 + lax.rem(i, 4), scale)
            return 0

        lax.fori_loop(0, 16, some, 0, unroll=8)

    def norm_sides(buf, scale):
        for inside, r in ((tile > 0, 0), (tile < tiles - 1, 5)):

            @pl.when(inside)
            def _(r=r):
                for f in range(2, 6):
                    norm_row(buf, f, r, scale)

    def norm_past(buf, f, scale):
        @pl.when(tm > 0)
        def _():
            for r in range(1, 5):
                norm_row(buf, f, r, scale)

        for inside, r in ((tile > 0, 0), (tile < tiles - 1, 5)):

            @pl.when(inside & (tm > 0))
            def _(r=r):
                norm_row(buf, f, r, scale)

    def mix(q):
        def some(r, _):
            d = [act[(2 - 2 * q + i) * 6 + r] for i in range(4)]
            mixed[r] = d[0] - d[2]
            mixed[6 + r] = d[1] + d[2]
            mixed[12 + r] = d[2] - d[1]
            mixed[18 + r] = d[1] - d[3]
            return 0

        lax.fori_loop(0, 6, some, 0, unroll=2)

    def product(taps, j):
        total = None
        for b in range(3):
            at = pl.ds(j * 6 + b, 4)
            piece = jnp.concatenate(
                [mixed[at, STEP * c : STEP * c + COLS, :].reshape(4 * COLS, 256) for c in range(3)], axis=1
            )
            term = mm(piece, taps[b].reshape(768, 256))
            total = term if total is None else total + term
        return total

    def direct(taps, units):
        total = None
        for o, a in units:
            for b in range(3):
                at = pl.ds((o + a) * 6 + b, 4)
                piece = jnp.concatenate(
                    [act[at, STEP * c : STEP * c + COLS, :].reshape(4 * COLS, 256) for c in range(3)], axis=1
                )
                term = mm(piece, taps[a, b].reshape(768, 256))
                total = term if total is None else total + term
        return total

    def conv(taps, blended, halo, buf, scale, done, between, arrived):
        mix(0)
        m1, m2 = product(blended.at[0], 1), product(blended.at[1], 2)
        y0, y1 = m1 + m2, m1 - m2
        acc[0] = y0 + product(taps.at[0], 0)
        acc[1] = y1 - product(taps.at[2], 3)
        carry = done(2, 0, (zero, zero))
        carry = done(2, 1, carry)
        between()
        acc[0] = direct(taps, ((0, 2),))
        acc[1] = direct(taps, ((1, 1), (1, 2)))
        received(halo.diagonal + halo.forward + halo.rest[1])
        norm_past(buf, 1, scale)
        received(halo.rest[0])
        arrived()
        norm_past(buf, 0, scale)
        acc[1] += direct(taps, ((1, 0),))
        acc[0] += direct(taps, ((0, 1), (0, 0)))
        return done(0, 1, done(0, 0, carry))

    scale = scales(totals1.end(), params[16:17], params[17:18])
    norm_own(first, scale)
    received(halo1.rows[4] + halo1.rows[2])
    norm_sides(first, scale)
    received(halo1.edge)
    start(halo1.forward)

    def keep(o, half, sums):
        hidden = acc[half].astype(BF16)
        second[2 + o + half, pl.ds(1, 4)] = hidden.reshape(4, COLS, 256)
        v = hidden.astype(F32).reshape(4 * COLS // 8, 8, 256)
        return sums[0] + v.sum(axis=0), sums[1] + (v * v).sum(axis=0)

    sums = conv(
        taps1, blend1, halo1, first, scale, keep, lambda: None, lambda: start(halo2.rows[4] + halo2.edge + halo2.diagonal)
    )

    totals2.begin(sums)
    start(halo2.rows[2])
    totals2.middle()
    start(halo2.rest[1] + halo2.rest[0])
    scale = scales(totals2.end(), params[18:19], params[19:20])
    norm_own(second, scale)
    received(halo2.rows[4] + halo2.rows[2])
    norm_sides(second, scale)
    received(halo2.edge)
    start(halo2.forward)

    def finish_latents(o, half):
        frames = first[2 + o, pl.ds(1, 4)].reshape(4 * COLS, 256).astype(F32)
        features = (frames + acc[half]).astype(BF16)
        final[o] = features.reshape(4, COLS, 256)
        latents = mm(features, latent[...])
        lane = iota((STEP, 256), 1) // 16
        for i in range(2):
            block = jnp.zeros((STEP, 256), F32)
            for p in range(2):
                for s in range(RUNS):
                    at = (2 * i + p) * COLS + s * STEP
                    here = lane == 4 * (s // 2) + 2 * p + s % 2
                    block = jnp.where(here, latents[at : at + STEP], block)
            rows[pl.ds(pl.multiple_of((2 * o + i) * STEP, STEP), STEP)] = block

    def finish_features(o):
        for r in range(4):
            feat[o, r] = mm(back[...], final[o, r]).astype(BF16)

    def finish(o, half, carry):
        finish_latents(o + half, half)
        return carry

    def finish_early():
        finish_features(3)
        finish_features(2)

    conv(taps2, blend2, halo2, second, scale, finish, finish_early, lambda: None)

    turn = (b == (a % 8) * 16 + a // 8).astype(F32).astype(BF16)
    outbox[...] = mm(turn, rows[...].astype(BF16)).reshape(16, 8, 256)
    copies = []
    for k in range(1, tiles):
        to = lax.rem(tile + k, tiles)
        copies.append(send(outbox.at[to], inbox.at[tile], ts.at[k], tr.at[k], dev(tm, to)))
    for copy in copies:
        copy.start()

    finish_features(1)
    finish_features(0)
    inbox[tile] = outbox[tile]
    turn = (b == ((a % 32) // 2) * 8 + (a // 32) * 2 + a % 2).astype(F32).astype(BF16)
    for k in range(1, tiles):
        source = lax.rem(tile + tiles - k, tiles)
        send(outbox.at[source], inbox.at[source], ts.at[k], tr.at[k], dev(tm, source)).wait_recv()
    tok[...] = mm(turn, inbox[...].reshape(128, 256).astype(BF16)).astype(BF16).reshape(4, 32, 256)
    for copy in copies:
        copy.wait_send()
    totals1.sent()
    totals2.sent()
    sent(halo1.all + halo2.all)


def body(frames, g1, b1, w1, g2, b2, w2, lw):
    hbm, vmem = pl.BlockSpec(memory_space=pltpu.HBM), pl.BlockSpec(memory_space=pltpu.VMEM)
    dma = pltpu.SemaphoreType.DMA
    params = jnp.concatenate([lw.T.astype(F32)] + [v.reshape(1, 256) for v in (g1, b1, g2, b2)], axis=0)
    return pl.pallas_call(
        kernel,
        out_shape=[
            jax.ShapeDtypeStruct((4, 4, 128, 256), BF16),
            jax.ShapeDtypeStruct((4, 32, 256), BF16),
        ],
        in_specs=[hbm, vmem, hbm, hbm],
        out_specs=[vmem, vmem],
        scratch_shapes=[
            pltpu.VMEM((4, 4, 128, 256), BF16),
            pltpu.VMEM((4, 4, 128, 256), BF16),
            pltpu.VMEM((6, 6, 128, 256), BF16),
            pltpu.VMEM((6, 6, 128, 256), BF16),
            pltpu.VMEM((36, 160, 256), BF16),
            pltpu.VMEM((24, 160, 256), BF16),
            pltpu.VMEM((2, 512, 256), F32),
            pltpu.VMEM((3, 3, 3, 256, 256), BF16),
            pltpu.VMEM((3, 3, 3, 256, 256), BF16),
            pltpu.VMEM((2, 3, 3, 256, 256), BF16),
            pltpu.VMEM((2, 3, 3, 256, 256), BF16),
            pltpu.VMEM((128, 256), F32),
            pltpu.VMEM((128, 128), BF16),
            pltpu.VMEM((128, 128), BF16),
            pltpu.VMEM((256, 256), BF16),
            pltpu.VMEM((256, 256), BF16),
            pltpu.VMEM((16, 8, 256), F32),
            pltpu.VMEM((16, 8, 256), F32),
            pltpu.VMEM((8, 512), F32),
            pltpu.VMEM((16, 512), F32),
            pltpu.VMEM((8, 512), F32),
            pltpu.VMEM((16, 512), F32),
            dma((11,)),
        ]
        + [dma((11,))] * 4
        + [dma((7,)), dma((7,)), dma((15,)), dma((15,))] * 2
        + [dma((16,)), dma((16,))],
        compiler_params=pltpu.CompilerParams(
            collective_id=0, has_side_effects=True, vmem_limit_bytes=54000 * 2**10
        ),
    )(frames, params, w1, w2)


def solution(mesh):
    return jax.shard_map(
        body,
        mesh=mesh,
        in_specs=(P("tm", "tile", None, None), P(), P(), P(), P(), P(), P(), P()),
        out_specs=(P("tm", "tile", None, None), P("tm", None, "tile")),
        check_vma=False,
    )
```
